32 devices in a mesh: groups: 2 (over y), rows: 8 (over z, x), cols: 2 (over core).
Axes of the slice: x: 2, y: 2, z: 4, core: 2. Of those that a mesh axis runs over, the one named last changes fastest.
Arguments:
- earlier_features: bfloat16 [64, 96, 1024], P(('groups', 'rows', 'cols')), parts along dimension 0, may hold values from -6 to 6
- later_features: bfloat16 [64, 96, 1024], P(('groups', 'rows', 'cols')), parts along dimension 0, may hold values from -6 to 6
- cotangent: bfloat16 [64, 128, 1024], P(('groups', 'rows', 'cols')), parts along dimension 0, may hold values from -6 to 6
- proj_weight: bfloat16 [162, 128], replicated, may hold values from -0.5 to 0.5
- owner_slot: int32 [64], P('groups'), parts along dimension 0, may hold values from 0 to 31, as said below
- neighbour_labels: int32 [64, 8], P(('groups', 'rows', 'cols')), parts along dimension 0, may hold values from -1 to 31, as said below
- disk_mask: int32 [64], P(('groups', 'rows', 'cols')), parts along dimension 0, may hold values from 0 to 1, as said below
Outputs:
- flow_features: bfloat16 [64, 128, 1024], P(('groups', 'rows', 'cols')), parts along dimension 0
- grad_first: bfloat16 [64, 96, 1024], P(('groups', 'rows', 'cols')), parts along dimension 0
- grad_second: bfloat16 [64, 96, 1024], P(('groups', 'rows', 'cols')), parts along dimension 0
- grad_proj: float32 [324, 128], P('groups'), parts along dimension 0
The draws below stay inside these ranges and needn't reach their ends.
There are 2 independent parts, one for each index of `groups`. The reference program is written for one: setup_inputs(seed, part) draws one part's arguments, and reference() takes and returns one part's arrays. A program takes and returns all parts, laid end to end along the dimension named above; an argument that names none is the same for every part. Nothing has to cross between parts.
Inputs may be any that keep to these rules, and one draw needn't show every extreme that they name: A permutation: owner_slot[l] is the slot holding the tile labelled l. The tiles form a grid of 8 rows by 4 columns; the device at rows index r and cols index c holds slots (2 * r + c) * 2 to (2 * r + c + 1) * 2 - 1, which carry tile row r and tile columns c * 2 to (c + 1) * 2 - 1 in an order of their own. `neighbour_labels`: for slot s and direction j, the label of the tile one step away in that direction on the tile grid, or -1 where that tile is outside the grid or off the disk. `disk_mask`: 1 where the slot's tile lies on the disk, a single circle over the tile grid; 0 elsewhere.
All inputs are finite; a program needn't handle non-finite values.
Results may differ from the reference program's by a relative error of at most 0.0049.
Values may be sent and summed in bfloat16 or wider, within the bound.
A program may use at most 256 MiB of HBM per device.

```python
import math
import jax
import jax.numpy as jnp
from jax import lax

FEATURE_CHANNELS = 96
PROJECTED_WIDTH = 128
TILE_SIDE = 32
RAD = 4
FINE_STEP1 = 2
COARSE_STEP2 = 1
SLOTS = 2
TILE_MARGIN = 8
LEVEL_OFFSETS = 81
Q = 162
TILE_ROWS = 8
TILE_COLS = 4
PAIR_TILES = 32


DIRECTIONS = ((-1, 0), (1, 0), (0, -1), (0, 1), (-1, -1), (-1, 1), (1, -1), (1, 1))


def tile_layout(key):
    split_keys = jax.random.split(key, 5)
    centre_row = TILE_ROWS + jax.random.randint(split_keys[0], (), -1, 2)
    centre_col = TILE_COLS + jax.random.randint(split_keys[1], (), -(TILE_COLS // 4), TILE_COLS // 4 + 1)
    diameter = TILE_ROWS - jax.random.randint(split_keys[2], (), 0, TILE_ROWS // 8 + 1)
    row_grid = jnp.broadcast_to(jnp.arange(TILE_ROWS, dtype=jnp.int32)[:, None], (TILE_ROWS, TILE_COLS))
    col_grid = jnp.broadcast_to(jnp.arange(TILE_COLS, dtype=jnp.int32)[None, :], (TILE_ROWS, TILE_COLS))
    within_disk = ((2 * row_grid + 1 - centre_row) ** 2 + (2 * col_grid + 1 - centre_col) ** 2 <= diameter ** 2).astype(jnp.int32)
    tile_labels = jax.random.permutation(split_keys[3], TILE_ROWS * TILE_COLS).astype(jnp.int32)
    label_grid = tile_labels.reshape(TILE_ROWS, TILE_COLS)
    col_groups = TILE_COLS // SLOTS
    device_keys = jax.random.split(split_keys[4], TILE_ROWS * col_groups)
    local_order = jax.vmap(lambda one_key: jax.random.permutation(one_key, SLOTS))(device_keys).astype(jnp.int32)
    device_grid = row_grid * col_groups + col_grid // SLOTS
    slot_grid = device_grid * SLOTS + local_order[device_grid, col_grid % SLOTS]
    flattened_slot = slot_grid.reshape(-1)
    owning_slot = jnp.zeros((PAIR_TILES,), jnp.int32).at[tile_labels].set(flattened_slot)
    columns = []
    for row_step, col_step in DIRECTIONS:
        near_row = row_grid + row_step
        near_col = col_grid + col_step
        in_grid = (near_row >= 0) & (near_row < TILE_ROWS) & (near_col >= 0) & (near_col < TILE_COLS)
        safe_row = jnp.clip(near_row, 0, TILE_ROWS - 1)
        safe_col = jnp.clip(near_col, 0, TILE_COLS - 1)
        on_disk = within_disk[safe_row, safe_col] == 1
        columns.append(jnp.where(in_grid & on_disk, label_grid[safe_row, safe_col], -1))
    neighbour_geometry = jnp.stack(columns, axis=-1).reshape(-1, 8).astype(jnp.int32)
    adjacent_slot = jnp.zeros((PAIR_TILES, 8), jnp.int32).at[flattened_slot].set(neighbour_geometry)
    slot_disk_mask = jnp.zeros((PAIR_TILES,), jnp.int32).at[flattened_slot].set(within_disk.reshape(-1))
    return (owning_slot, adjacent_slot, slot_disk_mask)


def draw_owner_slot(key, part):
    return tile_layout(key)[0]


def draw_neighbour_labels(key, part):
    return tile_layout(key)[1]


def draw_disk_mask(key, part):
    return tile_layout(key)[2]


def block_scale(rng, shape, cuts, low, top_value):
    def one(axis_at, parts):
        draws = jax.random.uniform(jax.random.fold_in(jax.random.fold_in(rng, 6), axis_at), (parts,), jnp.float32, low / len(cuts), top_value / len(cuts))
        return jnp.repeat(jnp.exp(draws), shape[axis_at] // parts).reshape((-1,) + (1,) * (len(shape) - axis_at - 1))

    gain = one(*cuts[0])
    for cut in cuts[1:]:
        gain = gain * one(*cut)
    return gain


def scatter_about(stream_key, shape, scale, limit, shards=(), kind=jnp.bfloat16):
    entries = jax.random.normal(stream_key, shape, jnp.float32) * scale
    if len(shards) > 0:
        entries = block_scale(stream_key, shape, shards, -0.22, 0.18) * entries
    return jnp.clip(entries, min=-limit, max=limit).astype(kind)


def setup_inputs(seed: int = 0, part: int = 0) -> dict:
    key_list = jax.random.split(jax.random.key(seed), 8)
    own_keys = jax.random.split(jax.random.fold_in(key_list[7], part), 8)
    earlier_features = scatter_about(own_keys[0], (PAIR_TILES, FEATURE_CHANNELS, TILE_SIDE * TILE_SIDE), 1.0, 6.0, ((0, 16),))
    later_features = scatter_about(own_keys[1], (PAIR_TILES, FEATURE_CHANNELS, TILE_SIDE * TILE_SIDE), 1.0, 6.0, ((0, 16),))
    cotangent = scatter_about(own_keys[2], (PAIR_TILES, PROJECTED_WIDTH, TILE_SIDE * TILE_SIDE), 1.0, 6.0, ((0, 16),))
    proj_weight = scatter_about(key_list[3], (Q, PROJECTED_WIDTH), Q ** -0.5, 0.5)
    owner_slot = draw_owner_slot(jax.random.fold_in(jax.random.fold_in(key_list[7], part), 71), part)
    neighbour_labels = draw_neighbour_labels(jax.random.fold_in(jax.random.fold_in(key_list[7], part), 71), part)
    disk_mask = draw_disk_mask(jax.random.fold_in(jax.random.fold_in(key_list[7], part), 71), part)
    return {"earlier_features": earlier_features, "later_features": later_features, "cotangent": cotangent, "proj_weight": proj_weight, "owner_slot": owner_slot, "neighbour_labels": neighbour_labels, "disk_mask": disk_mask}


DIRECTIONS = ((-1, 0), (1, 0), (0, -1), (0, 1), (-1, -1), (-1, 1), (1, -1), (1, 1))

def tile_span(step_value):
    return ((TILE_SIDE - TILE_MARGIN, TILE_SIDE), (0, TILE_SIDE), (0, TILE_MARGIN))[step_value + 1]

def margin_span(step_value):
    return ((0, TILE_MARGIN), (TILE_MARGIN, TILE_MARGIN + TILE_SIDE), (TILE_MARGIN + TILE_SIDE, TILE_SIDE + 2 * TILE_MARGIN))[step_value + 1]

def offsets(margin, dilation):
    shift_pairs = []
    for row_step in range(-RAD, RAD + 1):
        for col_step in range(-RAD, RAD + 1):
            shift_pairs.append((margin + dilation * row_step, margin + dilation * col_step))
    return shift_pairs

def averaged_features(field):
    tile_count, channel_count, height, field_width = field.shape
    return field.reshape(tile_count, channel_count, height // 2, 2, field_width // 2, 2).mean(axis=(3, 5))

def coarse_sum(field):
    tile_count, channel_count, height, field_width = field.shape
    return field.reshape(tile_count, channel_count, height // 2, 2, field_width // 2, 2).sum(axis=(3, 5))

def coarse_repeat(field):
    return jnp.repeat(jnp.repeat(field, 2, axis=2), 2, axis=3)

def window_correlations(query_patch, search_patch, margin, dilation):
    extent = query_patch.shape[2]
    values = [lax.optimization_barrier(jnp.sum(query_patch * search_patch[:, :, row_start:row_start + extent, col_start:col_start + extent], axis=1)) for row_start, col_start in offsets(margin, dilation)]
    return jnp.stack(values, axis=1) / math.sqrt(FEATURE_CHANNELS)

def window_gradients(query_patch, search_patch, grad_scores, margin, dilation):
    extent = query_patch.shape[2]
    grad_query = jnp.zeros_like(query_patch)
    grad_search = jnp.zeros_like(search_patch)
    for number, (row_start, col_start) in enumerate(offsets(margin, dilation)):
        weight_map = grad_scores[:, number, None, :, :] / math.sqrt(FEATURE_CHANNELS)
        grad_query = grad_query + weight_map * search_patch[:, :, row_start:row_start + extent, col_start:col_start + extent]
        grad_search = grad_search.at[:, :, row_start:row_start + extent, col_start:col_start + extent].add(weight_map * query_patch)
    return (grad_query, grad_search)

def correlate(query_patch, search_patch):
    tile_count = query_patch.shape[0]
    fine_level = window_correlations(query_patch, search_patch, TILE_MARGIN, FINE_STEP1)
    coarse_level = coarse_repeat(window_correlations(averaged_features(query_patch), averaged_features(search_patch), TILE_MARGIN // 2, COARSE_STEP2))
    return jnp.concatenate([fine_level, coarse_level], axis=1).reshape(tile_count, 2 * LEVEL_OFFSETS, TILE_SIDE * TILE_SIDE)

def correlate_grads(query_patch, search_patch, grad_scores):
    tile_count = query_patch.shape[0]
    gradient_grid = grad_scores.reshape(tile_count, 2 * LEVEL_OFFSETS, TILE_SIDE, TILE_SIDE)
    fine_query, fine_search = window_gradients(query_patch, search_patch, gradient_grid[:, :LEVEL_OFFSETS], TILE_MARGIN, FINE_STEP1)
    coarse_query, coarse_search = window_gradients(averaged_features(query_patch), averaged_features(search_patch), coarse_sum(gradient_grid[:, LEVEL_OFFSETS:]), TILE_MARGIN // 2, COARSE_STEP2)
    return (fine_query + coarse_repeat(coarse_query) / 4.0, fine_search + coarse_repeat(coarse_search) / 4.0)

def assemble(centre_tile, neighbour_parts):
    band_rows = []
    for row_step in (-1, 0, 1):
        band_parts = []
        for col_step in (-1, 0, 1):
            if row_step == 0 and col_step == 0:
                band_parts.append(centre_tile)
            else:
                band_parts.append(neighbour_parts[DIRECTIONS.index((row_step, col_step))])
        band_rows.append(jnp.concatenate(band_parts, axis=3))
    return jnp.concatenate(band_rows, axis=2)

def reference(earlier_features, later_features, cotangent, proj_weight, owner_slot, neighbour_labels, disk_mask):
    total_slots = earlier_features.shape[0]
    slot_mask = disk_mask.astype(jnp.float32)[:, None, None, None]
    first_tiles = (earlier_features.reshape(total_slots, FEATURE_CHANNELS, TILE_SIDE, TILE_SIDE) * slot_mask).astype(jnp.bfloat16)
    second_tiles = (later_features.reshape(total_slots, FEATURE_CHANNELS, TILE_SIDE, TILE_SIDE) * slot_mask).astype(jnp.bfloat16)
    present = neighbour_labels >= 0
    near_all = owner_slot[jnp.where(present, neighbour_labels, 0)].astype(jnp.int32)
    presence_all = present.astype(jnp.float32)
    weight_wide = proj_weight.astype(jnp.float32)
    block_total = total_slots // SLOTS

    def scan_step(carried, block_index):
        second_acc, proj_acc = carried
        block_start = (block_index * SLOTS).astype(jnp.int32)
        own_tiles = lax.dynamic_slice_in_dim(second_tiles, block_start, SLOTS, 0)
        query_block = lax.dynamic_slice_in_dim(first_tiles, block_start, SLOTS, 0)
        mask_block = lax.dynamic_slice_in_dim(slot_mask, block_start, SLOTS, 0)
        near_slots = lax.dynamic_slice_in_dim(near_all, block_start, SLOTS, 0)
        near_present = lax.dynamic_slice_in_dim(presence_all, block_start, SLOTS, 0)
        cot_block = lax.dynamic_slice_in_dim(cotangent, block_start, SLOTS, 0)
        neighbour_parts = {}
        for direction_index, (row_step, col_step) in enumerate(DIRECTIONS):
            picked_tile = jnp.take(second_tiles, near_slots[:, direction_index], axis=0)
            row_low, row_high = tile_span(row_step)
            col_low, col_high = tile_span(col_step)
            keep_flag = near_present[:, direction_index, None, None, None].astype(jnp.bfloat16)
            neighbour_parts[direction_index] = picked_tile[:, :, row_low:row_high, col_low:col_high] * keep_flag
        extended = assemble(own_tiles, neighbour_parts)
        query_wide = query_block.astype(jnp.float32)
        search_wide = extended.astype(jnp.float32)
        correlation = lax.optimization_barrier(correlate(query_wide, search_wide).astype(jnp.bfloat16))
        corr_wide = correlation.astype(jnp.float32)
        cot_wide = cot_block.astype(jnp.float32)
        flow_block = jnp.einsum('qp,sqn->spn', weight_wide, corr_wide).astype(jnp.bfloat16)
        grad_correlation = jnp.einsum('qp,spn->sqn', weight_wide, cot_wide)
        proj_acc = proj_acc + jnp.einsum('sqn,spn->qp', corr_wide, cot_wide)
        grad_query, grad_extended = correlate_grads(query_wide, search_wide, grad_correlation)
        centre_grad = grad_extended[:, :, TILE_MARGIN:TILE_MARGIN + TILE_SIDE, TILE_MARGIN:TILE_MARGIN + TILE_SIDE]
        current = lax.dynamic_slice_in_dim(second_acc, block_start, SLOTS, 0)
        second_acc = lax.dynamic_update_slice_in_dim(second_acc, current + centre_grad, block_start, 0)
        for direction_index, (row_step, col_step) in enumerate(DIRECTIONS):
            edge_low, edge_high = margin_span(row_step)
            side_low, side_high = margin_span(col_step)
            keep_flag = near_present[:, direction_index, None, None, None]
            rim_part = grad_extended[:, :, edge_low:edge_high, side_low:side_high] * keep_flag
            rim_part = lax.optimization_barrier(rim_part.astype(jnp.bfloat16)).astype(jnp.float32)
            row_low, row_high = tile_span(row_step)
            col_low, col_high = tile_span(col_step)
            second_acc = second_acc.at[near_slots[:, direction_index], :, row_low:row_high, col_low:col_high].add(rim_part)
        first_block = (grad_query * mask_block).astype(jnp.bfloat16)
        return ((second_acc, proj_acc), (flow_block, first_block))
    start_state = (jnp.zeros((total_slots, FEATURE_CHANNELS, TILE_SIDE, TILE_SIDE), jnp.float32), jnp.zeros((2 * LEVEL_OFFSETS, PROJECTED_WIDTH), jnp.float32))
    (second_acc, proj_acc), (flow_blocks, first_blocks) = lax.scan(scan_step, start_state, jnp.arange(block_total, dtype=jnp.int32))
    flow_features = flow_blocks.reshape(total_slots, PROJECTED_WIDTH, TILE_SIDE * TILE_SIDE)
    grad_first = first_blocks.reshape(total_slots, FEATURE_CHANNELS, TILE_SIDE * TILE_SIDE)
    grad_second = (second_acc * slot_mask).astype(jnp.bfloat16).reshape(total_slots, FEATURE_CHANNELS, TILE_SIDE * TILE_SIDE)
    grad_proj = proj_acc / math.sqrt(total_slots * TILE_SIDE * TILE_SIDE)
    return (flow_features, grad_first, grad_second, grad_proj)
```

```python
import math

import jax
import jax.numpy as jnp
from jax import lax
from jax.experimental import pallas as pl
from jax.experimental.pallas import tpu as pltpu
from jax.sharding import PartitionSpec as P

CHANNELS = 96
WIDTH = 128
GRID = 16
STRIP = 32
MARGIN = 4
WINDOW = 9
PITCH = 48
LANES = 512
EXT_ROWS = (GRID - 1) * PITCH + LANES
SCALE = 1.0 / math.sqrt(CHANNELS)
F32 = jnp.float32
BF16 = jnp.bfloat16
NT = (((1,), (1,)), ((), ()))
NN = (((1,), (0,)), ((), ()))
TN = (((0,), (0,)), ((), ()))


def dot(a, b, dims):
    return lax.dot_general(a, b, dims, preferred_element_type=F32)


def permutation(backwards):
    o = lax.broadcasted_iota(jnp.int32, (256, 256), 0)
    i = lax.broadcasted_iota(jnp.int32, (256, 256), 1)
    y = 2 * ((o >> 4) & 3) + (o >> 7)
    col = 15 - (o & 15) if backwards else o & 15
    x = 2 * col + ((o >> 6) & 1)
    return jnp.where(i == y * 32 + x, 1.0, 0.0).astype(BF16)


def left_slot(owner_ref, labels_ref):
    base = (lax.axis_index("rows") * lax.axis_size("cols") + lax.axis_index("cols")) * 2
    right_of = labels_ref[0, 3]
    left_of = labels_ref[1, 2]
    first = (right_of >= 0) & (owner_ref[jnp.maximum(right_of, 0)] == base + 1)
    second = (left_of >= 0) & (owner_ref[jnp.maximum(left_of, 0)] == base)
    return jnp.where(first | second, 0, 1)


def strip_rows(blk, row, half):
    return pl.ds((blk * 4 + row) * STRIP + half * 16, 16)


def split_kernel(owner, labels, mask, perm, earlier, later, cot, q_out, e_out, c_out, q_back, c_back, side, upc, downc):
    left = left_slot(owner, labels)
    col = lax.axis_index("cols")
    for half in range(2):
        slot = left if half == 0 else 1 - left
        keep = mask[slot].astype(F32)
        for blk in range(4):
            cols = slice(blk * 256, blk * 256 + 256)
            for src, dst, masked, order in (
                (earlier, q_out, True, 0),
                (later, e_out, True, 0),
                (cot, c_out, False, 0),
                (earlier, q_back, True, 1),
                (cot, c_back, False, 1),
            ):
                at = half ^ order
                tile = src[slot, :, cols]
                if src is not cot:
                    tile = jnp.concatenate([tile, jnp.zeros((WIDTH - CHANNELS, 256), BF16)], axis=0)
                v = dot(perm[order], tile, NT)
                if masked:
                    v = v * keep
                w = v.astype(BF16)
                for k in range(4):
                    for row in range(4):
                        r = k * 64 + row * 16
                        dst[k, strip_rows(blk, row, at), :] = w[r : r + 16]
                if src is not later:
                    s = v[:64] + v[64:128] + v[128:192] + v[192:]
                    if masked:
                        s = s * 0.25
                    s = s.astype(BF16)
                    for row in range(4):
                        dst[4, strip_rows(blk, row, at), :] = s[row * 16 : row * 16 + 16]
    sub = lax.broadcasted_iota(jnp.int32, (16, WIDTH), 0)
    edge = jnp.where(col == 0, (sub >= 12).astype(F32), (sub < 4).astype(F32)).astype(BF16)
    for k in range(4):
        for row in range(GRID):
            lo = e_out[k, row * STRIP : row * STRIP + 16, :]
            hi = e_out[k, row * STRIP + 16 : row * STRIP + 32, :]
            v = jnp.where(col == 0, hi, lo) * edge
            side[k, row * 16 : row * 16 + 16, :] = v
            if row < MARGIN:
                upc[k, row * 16 : row * 16 + 16, :] = v
            if row >= GRID - MARGIN:
                downc[k, (row - 12) * 16 : (row - 12) * 16 + 16, :] = v


def ext_row(row):
    return pl.multiple_of(row * PITCH, 16)


def forward_kernel(perm, w_ref, q, e, above, below, side, above_side, below_side, c, left_ref,
                   ext, flow, proj, skew, flow_t, coarse):
    col = lax.axis_index("cols")
    ext[...] = jnp.zeros_like(ext)
    for k in range(4):
        for row in range(GRID + 2 * MARGIN):
            if row < MARGIN:
                src, sd, at = above, above_side, row
            elif row < GRID + MARGIN:
                src, sd, at = e, side, row - MARGIN
            else:
                src, sd, at = below, below_side, row - GRID - MARGIN
            ext[k, 16 + row * PITCH : 16 + row * PITCH + 32, :] = src[k, at * STRIP : at * STRIP + 32, :]
            ext[k, pl.ds(ext_row(row + 1 - col), 16), :] = sd[k, at * 16 : at * 16 + 16, :]
    for i in range(0, EXT_ROWS, 176):
        rows = slice(i, i + 176)
        s = sum(ext[k, rows, :].astype(F32) for k in range(4)) * 0.25
        ext[4, rows, :] = s.astype(BF16)

    def step(row, carry):
        qr = pl.ds(pl.multiple_of(row * STRIP, 32), STRIP)
        er = pl.ds(ext_row(row), LANES)
        for k in range(5):
            s = dot(q[k, qr, :], ext[k, er, :], NT) * SCALE
            s = pltpu.roll(s, 0, 1, stride=1, stride_axis=0)
            skew[k, qr, :] = s.astype(BF16)
        return carry

    lax.fori_loop(0, GRID, step, 0)

    def project(chunk, carry):
        rows = pl.ds(pl.multiple_of(chunk * 128, 128), 128)
        coarse[...] = dot(skew[4, rows, :], w_ref[1], NN)
        for k in range(4):
            flow_t[k, rows, :] = (dot(skew[k, rows, :], w_ref[0], NN) + coarse[...]).astype(BF16)
        return carry

    lax.fori_loop(0, 4, project, 0)
    acc = jnp.zeros((LANES, WIDTH), F32)
    for k in range(4):
        acc = acc + dot(skew[k], c[k], TN)
    acc2 = dot(skew[4], c[4], TN)
    for u in range(WINDOW):
        lo = u * PITCH + 12 + STRIP - 1
        proj[u * 9 : u * 9 + 9, :] = acc[lo : lo + 9]
        proj[81 + u * 9 : 81 + u * 9 + 9, :] = acc2[lo : lo + 9]
    join(perm[1], flow_t, flow, left_ref[0], None, 1)


def join(p, src, dst, left, mask, order=0):
    for half in range(2):
        slot = left if half == 0 else 1 - left
        for blk in range(4):
            v = jnp.concatenate(
                [src[k, strip_rows(blk, row, half ^ order), :] for k in range(4) for row in range(4)], axis=0
            )
            if mask is not None:
                v = v.astype(F32) * mask[slot].astype(F32)
            out = dot(v.astype(BF16), p, TN)
            dst[slot, :, blk * 256 : blk * 256 + 256] = out[: dst.shape[1]].astype(BF16)


def backward_kernel(perm, w_ref, q, ext, c, left_ref, mask,
                    g_first, centre, up, down, side, up_side, down_side, gext, gsc, gq):
    col = lax.axis_index("cols")
    gext[...] = jnp.zeros_like(gext)
    for k in range(5):
        gsc[k] = dot(c[k], w_ref[k // 4], NT) * SCALE

    def step(row, carry):
        qr = pl.ds(pl.multiple_of(row * STRIP, 32), STRIP)
        er = pl.ds(ext_row(row), LANES)
        terms = []
        for k in range(5):
            g = pltpu.roll(gsc[k, qr, :], 0, 1, stride=1, stride_axis=0).astype(BF16)
            terms.append(dot(g, ext[k, er, :], NN))
            gext[k, er, :] += dot(g, q[k, qr, :], TN)
        for k in range(4):
            gq[k, qr, :] = terms[k] + 0.25 * terms[4]
        return carry

    lax.fori_loop(0, GRID, step, 0)
    sub = lax.broadcasted_iota(jnp.int32, (16, WIDTH), 0)
    edge = jnp.where(col == 0, (sub < 4).astype(F32), (sub >= 12).astype(F32))
    for row in range(GRID + 2 * MARGIN):
        lo = 16 + row * PITCH
        er = pl.ds(ext_row(row + 1 - col), 16)
        coarse = 0.25 * gext[4, lo : lo + 32, :]
        coarse_side = 0.25 * gext[4, er, :]
        for k in range(4):
            v = gext[k, lo : lo + 32, :] + coarse
            s = ((gext[k, er, :] + coarse_side) * edge).astype(BF16)
            if row < MARGIN:
                up[k, row * 32 : row * 32 + 32, :] = v.astype(BF16)
                up_side[k, row * 16 : row * 16 + 16, :] = s
            elif row < GRID + MARGIN:
                at = row - MARGIN
                centre[k, at * 32 : at * 32 + 32, :] = v
                side[k, at * 16 : at * 16 + 16, :] = s
            else:
                at = row - GRID - MARGIN
                down[k, at * 32 : at * 32 + 32, :] = v.astype(BF16)
                down_side[k, at * 16 : at * 16 + 16, :] = s
    join(perm[0], gq, g_first, left_ref[0], mask)


def finish_kernel(perm, left_ref, mask, centre, above, below, side, above_side, below_side, g_second, total):
    col = lax.axis_index("cols")
    place = pl.multiple_of((1 - col) * 16, 16)
    total[...] = centre[...]
    for k in range(4):
        for row in range(GRID):
            rows = pl.ds(row * 32, 32)
            part = pl.ds(row * 32 + place, 16)
            sd = side[k, row * 16 : row * 16 + 16, :].astype(F32)
            if row < MARGIN:
                total[k, rows, :] += above[k, row * 32 : row * 32 + 32, :].astype(F32)
                sd = sd + above_side[k, row * 16 : row * 16 + 16, :].astype(F32)
            if row >= GRID - MARGIN:
                at = row - GRID + MARGIN
                total[k, rows, :] += below[k, at * 32 : at * 32 + 32, :].astype(F32)
                sd = sd + below_side[k, at * 16 : at * 16 + 16, :].astype(F32)
            total[k, part, :] += sd
    join(perm[0], total, g_second, left_ref[0], mask)


def vm():
    return pl.BlockSpec(memory_space=pltpu.VMEM)


def sm():
    return pl.BlockSpec(memory_space=pltpu.SMEM)


def sds(shape, dtype):
    return jax.ShapeDtypeStruct(shape, dtype)


PARAMS = pltpu.CompilerParams(vmem_limit_bytes=48 * 1024 * 1024)


def shards(earlier, later, cot, weight, owner, labels, mask):
    rows = lax.axis_size("rows")
    cols = lax.axis_size("cols")
    base = (lax.axis_index("rows") * cols + lax.axis_index("cols")) * 2
    right_of = labels[0, 3]
    left_of = labels[1, 2]
    is_first = ((right_of >= 0) & (owner[jnp.maximum(right_of, 0)] == base + 1)) | (
        (left_of >= 0) & (owner[jnp.maximum(left_of, 0)] == base)
    )
    left = jnp.where(is_first, 0, 1).astype(jnp.int32)[None]
    perm = jnp.stack([permutation(False), permutation(True)])
    wide = jnp.pad(weight.reshape(2, 9, 9, WIDTH), ((0, 0), (0, 0), (0, PITCH - 9), (0, 0)))
    wide = wide.reshape(2, 9 * PITCH, WIDTH)
    wide, wide_back = (
        jnp.pad(wide, ((0, 0), (lo, LANES - 9 * PITCH - lo), (0, 0))) for lo in (12, 12 + STRIP - 1)
    )

    pos = GRID * STRIP
    q, e, c, q_back, c_back, side, upc, downc = pl.pallas_call(
        split_kernel,
        out_shape=(
            sds((5, pos, WIDTH), BF16),
            sds((4, pos, WIDTH), BF16),
            sds((5, pos, WIDTH), BF16),
            sds((5, pos, WIDTH), BF16),
            sds((5, pos, WIDTH), BF16),
            sds((4, GRID * 16, WIDTH), BF16),
            sds((4, MARGIN * 16, WIDTH), BF16),
            sds((4, MARGIN * 16, WIDTH), BF16),
        ),
        in_specs=[sm(), sm(), sm(), vm(), vm(), vm(), vm()],
        out_specs=(vm(),) * 8,
        compiler_params=PARAMS,
    )(owner, labels, mask, perm, earlier, later, cot)

    up_pairs = [(i + 1, i) for i in range(rows - 1)]
    down_pairs = [(i, i + 1) for i in range(rows - 1)]
    cross = [(0, 1), (1, 0)]

    def diagonal(pairs):
        return [(a * cols + x, b * cols + y) for a, b in pairs for x, y in cross]

    def exchange(up, down, side, up_side, down_side):
        return (
            lax.ppermute(down, "rows", down_pairs),
            lax.ppermute(up, "rows", up_pairs),
            lax.ppermute(side, "cols", cross),
            lax.ppermute(down_side, ("rows", "cols"), diagonal(down_pairs)),
            lax.ppermute(up_side, ("rows", "cols"), diagonal(up_pairs)),
        )

    halo = exchange(e[:, : MARGIN * STRIP], e[:, pos - MARGIN * STRIP :], side, upc, downc)
    ext, flow, proj = pl.pallas_call(
        forward_kernel,
        out_shape=(
            sds((5, EXT_ROWS, WIDTH), BF16),
            sds((2, WIDTH, 1024), BF16),
            sds((162, WIDTH), F32),
        ),
        in_specs=[vm()] * 10 + [sm()],
        out_specs=(vm(),) * 3,
        scratch_shapes=[pltpu.VMEM((5, pos, LANES), BF16), pltpu.VMEM((4, pos, WIDTH), BF16), pltpu.VMEM((128, WIDTH), F32)],
        compiler_params=PARAMS,
    )(perm, wide_back, q_back, e, *halo, c_back, left)
    proj = lax.psum(proj, ("rows", "cols")) * (1.0 / math.sqrt(2 * rows * cols * 1024))
    rim = (4, MARGIN * STRIP, WIDTH)
    corner = (4, MARGIN * 16, WIDTH)
    g_first, centre, *rims = pl.pallas_call(
        backward_kernel,
        out_shape=(
            sds((2, CHANNELS, 1024), BF16),
            sds((4, pos, WIDTH), F32),
            sds(rim, BF16),
            sds(rim, BF16),
            sds((4, GRID * 16, WIDTH), BF16),
            sds(corner, BF16),
            sds(corner, BF16),
        ),
        in_specs=[vm()] * 5 + [sm()] * 2,
        out_specs=(vm(),) * 7,
        scratch_shapes=[
            pltpu.VMEM((5, EXT_ROWS, WIDTH), F32),
            pltpu.VMEM((5, pos, LANES), F32),
            pltpu.VMEM((4, pos, WIDTH), F32),
        ],
        compiler_params=PARAMS,
    )(perm, wide, q, ext, c, left, mask)
    got_above, got_below, got_side, got_above_side, got_below_side = exchange(*rims)
    g_second = pl.pallas_call(
        finish_kernel,
        out_shape=sds((2, CHANNELS, 1024), BF16),
        in_specs=[vm(), sm(), sm()] + [vm()] * 6,
        out_specs=vm(),
        scratch_shapes=[pltpu.VMEM((4, pos, WIDTH), F32)],
        compiler_params=PARAMS,
    )(perm, left, mask, centre, got_above, got_below, got_side, got_above_side, got_below_side)
    return flow, g_first, g_second, proj


def solution(mesh):
    spec = P(("groups", "rows", "cols"), None, None)
    return jax.shard_map(
        shards,
        mesh=mesh,
        in_specs=(spec, spec, spec, P(), P("groups"), P(("groups", "rows", "cols"), None), P(("groups", "rows", "cols"))),
        out_specs=(spec, spec, spec, P("groups", None)),
        check_vma=False,
    )
```

```python
import math

import jax
import jax.numpy as jnp
from jax import lax
from jax.experimental import pallas as pl
from jax.experimental.pallas import tpu as pltpu
from jax.sharding import PartitionSpec as P

CHANNELS = 96
WIDTH = 128
GRID = 16
STRIP = 32
MARGIN = 4
WINDOW = 9
PITCH = 48
LANES = 512
EXT_ROWS = (GRID - 1) * PITCH + LANES
SCALE = 1.0 / math.sqrt(CHANNELS)
F32 = jnp.float32
BF16 = jnp.bfloat16
NT = (((1,), (1,)), ((), ()))
NN = (((1,), (0,)), ((), ()))
TN = (((0,), (0,)), ((), ()))


def dot(a, b, dims):
    return lax.dot_general(a, b, dims, preferred_element_type=F32)


def permutation(backwards):
    o = lax.broadcasted_iota(jnp.int32, (256, 256), 0)
    i = lax.broadcasted_iota(jnp.int32, (256, 256), 1)
    y = 2 * ((o >> 4) & 3) + (o >> 7)
    col = 15 - (o & 15) if backwards else o & 15
    x = 2 * col + ((o >> 6) & 1)
    return jnp.where(i == y * 32 + x, 1.0, 0.0).astype(BF16)


def left_slot(owner_ref, labels_ref):
    base = (lax.axis_index("rows") * lax.axis_size("cols") + lax.axis_index("cols")) * 2
    right_of = labels_ref[0, 3]
    left_of = labels_ref[1, 2]
    first = (right_of >= 0) & (owner_ref[jnp.maximum(right_of, 0)] == base + 1)
    second = (left_of >= 0) & (owner_ref[jnp.maximum(left_of, 0)] == base)
    return jnp.where(first | second, 0, 1)


def strip_rows(blk, row, half):
    return pl.ds((blk * 4 + row) * STRIP + half * 16, 16)


def split_kernel(owner, labels, mask, perm, earlier, later, cot, q_out, e_out, c_out, q_back, c_back, side, upc, downc):
    left = left_slot(owner, labels)
    col = lax.axis_index("cols")
    for half in range(2):
        slot = left if half == 0 else 1 - left
        keep = mask[slot].astype(F32)
        for blk in range(4):
            cols = slice(blk * 256, blk * 256 + 256)
            for src, dst, masked, order in (
                (earlier, q_out, True, 0),
                (later, e_out, True, 0),
                (cot, c_out, False, 0),
                (earlier, q_back, True, 1),
                (cot, c_back, False, 1),
            ):
                at = half ^ order
                tile = src[slot, :, cols]
                if src is not cot:
                    tile = jnp.concatenate([tile, jnp.zeros((WIDTH - CHANNELS, 256), BF16)], axis=0)
                v = dot(perm[order], tile, NT)
                if masked:
                    v = v * keep
                w = v.astype(BF16)
                for k in range(4):
                    for row in range(4):
                        r = k * 64 + row * 16
                        dst[k, strip_rows(blk, row, at), :] = w[r : r + 16]
                if src is not later:
                    s = v[:64] + v[64:128] + v[128:192] + v[192:]
                    if masked:
                        s = s * 0.25
                    s = s.astype(BF16)
                    for row in range(4):
                        dst[4, strip_rows(blk, row, at), :] = s[row * 16 : row * 16 + 16]
    sub = lax.broadcasted_iota(jnp.int32, (16, WIDTH), 0)
    edge = jnp.where(col == 0, (sub >= 12).astype(F32), (sub < 4).astype(F32)).astype(BF16)
    for k in range(4):
        for row in range(GRID):
            lo = e_out[k, row * STRIP : row * STRIP + 16, :]
            hi = e_out[k, row * STRIP + 16 : row * STRIP + 32, :]
            v = jnp.where(col == 0, hi, lo) * edge
            side[k, row * 16 : row * 16 + 16, :] = v
            if row < MARGIN:
                upc[k, row * 16 : row * 16 + 16, :] = v
            if row >= GRID - MARGIN:
                downc[k, (row - 12) * 16 : (row - 12) * 16 + 16, :] = v


def ext_row(row):
    return pl.multiple_of(row * PITCH, 16)


def forward_kernel(perm, w_ref, q, e, above, below, side, above_side, below_side, c, left_ref,
                   ext, flow, proj, skew, flow_t, coarse):
    col = lax.axis_index("cols")
    ext[...] = jnp.zeros_like(ext)
    for k in range(4):
        for row in range(GRID + 2 * MARGIN):
            if row < MARGIN:
                src, sd, at = above, above_side, row
            elif row < GRID + MARGIN:
                src, sd, at = e, side, row - MARGIN
            else:
                src, sd, at = below, below_side, row - GRID - MARGIN
            ext[k, 16 + row * PITCH : 16 + row * PITCH + 32, :] = src[k, at * STRIP : at * STRIP + 32, :]
            ext[k, pl.ds(ext_row(row + 1 - col), 16), :] = sd[k, at * 16 : at * 16 + 16, :]
    for i in range(0, EXT_ROWS, 176):
        rows = slice(i, i + 176)
        s = sum(ext[k, rows, :].astype(F32) for k in range(4)) * 0.25
        ext[4, rows, :] = s.astype(BF16)

    def step(row, carry):
        qr = pl.ds(pl.multiple_of(row * STRIP, 32), STRIP)
        er = pl.ds(ext_row(row), LANES)
        for k in range(5):
            s = dot(q[k, qr, :], ext[k, er, :], NT) * SCALE
            s = pltpu.roll(s, 0, 1, stride=1, stride_axis=0)
            skew[k, qr, :] = s.astype(BF16)
        return carry

    lax.fori_loop(0, GRID, step, 0)

    def project(chunk, carry):
        rows = pl.ds(pl.multiple_of(chunk * 128, 128), 128)
        coarse[...] = dot(skew[4, rows, :], w_ref[1], NN)
        for k in range(4):
            flow_t[k, rows, :] = (dot(skew[k, rows, :], w_ref[0], NN) + coarse[...]).astype(BF16)
        return carry

    lax.fori_loop(0, 4, project, 0)
    acc = jnp.zeros((LANES, WIDTH), F32)
    for k in range(4):
        acc = acc + dot(skew[k], c[k], TN)
    acc2 = dot(skew[4], c[4], TN)
    for u in range(WINDOW):
        lo = u * PITCH + 12 + STRIP - 1
        proj[u * 9 : u * 9 + 9, :] = acc[lo : lo + 9]
        proj[81 + u * 9 : 81 + u * 9 + 9, :] = acc2[lo : lo + 9]
    join(perm[1], flow_t, flow, left_ref[0], None, 1)


def join(p, src, dst, left, mask, order=0):
    for half in range(2):
        slot = left if half == 0 else 1 - left
        for blk in range(4):
            v = jnp.concatenate(
                [src[k, strip_rows(blk, row, half ^ order), :] for k in range(4) for row in range(4)], axis=0
            )
            if mask is not None:
                v = v.astype(F32) * mask[slot].astype(F32)
            out = dot(v.astype(BF16), p, TN)
            dst[slot, :, blk * 256 : blk * 256 + 256] = out[: dst.shape[1]].astype(BF16)


def backward_kernel(perm, w_ref, q, ext, c, left_ref, mask,
                    g_first, centre, up, down, side, up_side, down_side, gext, gsc, gq):
    col = lax.axis_index("cols")
    gext[...] = jnp.zeros_like(gext)
    for k in range(5):
        gsc[k] = dot(c[k], w_ref[k // 4], NT) * SCALE

    def step(row, carry):
        qr = pl.ds(pl.multiple_of(row * STRIP, 32), STRIP)
        er = pl.ds(ext_row(row), LANES)
        terms = []
        for k in range(5):
            g = pltpu.roll(gsc[k, qr, :], 0, 1, stride=1, stride_axis=0).astype(BF16)
            terms.append(dot(g, ext[k, er, :], NN))
            gext[k, er, :] += dot(g, q[k, qr, :], TN)
        for k in range(4):
            gq[k, qr, :] = terms[k] + 0.25 * terms[4]
        return carry

    lax.fori_loop(0, GRID, step, 0)
    sub = lax.broadcasted_iota(jnp.int32, (16, WIDTH), 0)
    edge = jnp.where(col == 0, (sub < 4).astype(F32), (sub >= 12).astype(F32))
    for row in range(GRID + 2 * MARGIN):
        lo = 16 + row * PITCH
        er = pl.ds(ext_row(row + 1 - col), 16)
        coarse = 0.25 * gext[4, lo : lo + 32, :]
        coarse_side = 0.25 * gext[4, er, :]
        for k in range(4):
            v = gext[k, lo : lo + 32, :] + coarse
            s = ((gext[k, er, :] + coarse_side) * edge).astype(BF16)
            if row < MARGIN:
                up[k, row * 32 : row * 32 + 32, :] = v.astype(BF16)
                up_side[k, row * 16 : row * 16 + 16, :] = s
            elif row < GRID + MARGIN:
                at = row - MARGIN
                centre[k, at * 32 : at * 32 + 32, :] = v
                side[k, at * 16 : at * 16 + 16, :] = s
            else:
                at = row - GRID - MARGIN
                down[k, at * 32 : at * 32 + 32, :] = v.astype(BF16)
                down_side[k, at * 16 : at * 16 + 16, :] = s
    join(perm[0], gq, g_first, left_ref[0], mask)


def finish_kernel(perm, left_ref, mask, centre, above, below, side, above_side, below_side, g_second, total):
    col = lax.axis_index("cols")
    place = pl.multiple_of((1 - col) * 16, 16)
    total[...] = centre[...]
    for k in range(4):
        for row in range(GRID):
            rows = pl.ds(row * 32, 32)
            part = pl.ds(row * 32 + place, 16)
            sd = side[k, row * 16 : row * 16 + 16, :].astype(F32)
            if row < MARGIN:
                total[k, rows, :] += above[k, row * 32 : row * 32 + 32, :].astype(F32)
                sd = sd + above_side[k, row * 16 : row * 16 + 16, :].astype(F32)
            if row >= GRID - MARGIN:
                at = row - GRID + MARGIN
                total[k, rows, :] += below[k, at * 32 : at * 32 + 32, :].astype(F32)
                sd = sd + below_side[k, at * 16 : at * 16 + 16, :].astype(F32)
            total[k, part, :] += sd
    join(perm[0], total, g_second, left_ref[0], mask)


def vm():
    return pl.BlockSpec(memory_space=pltpu.VMEM)


def sm():
    return pl.BlockSpec(memory_space=pltpu.SMEM)


def sds(shape, dtype):
    return jax.ShapeDtypeStruct(shape, dtype)


PARAMS = pltpu.CompilerParams(vmem_limit_bytes=48 * 1024 * 1024)


def shards(earlier, later, cot, weight, owner, labels, mask):
    rows = lax.axis_size("rows")
    cols = lax.axis_size("cols")
    base = (lax.axis_index("rows") * cols + lax.axis_index("cols")) * 2
    right_of = labels[0, 3]
    left_of = labels[1, 2]
    is_first = ((right_of >= 0) & (owner[jnp.maximum(right_of, 0)] == base + 1)) | (
        (left_of >= 0) & (owner[jnp.maximum(left_of, 0)] == base)
    )
    left = jnp.where(is_first, 0, 1).astype(jnp.int32)[None]
    perm = jnp.stack([permutation(False), permutation(True)])
    wide = jnp.pad(weight.reshape(2, 9, 9, WIDTH), ((0, 0), (0, 0), (0, PITCH - 9), (0, 0)))
    wide = wide.reshape(2, 9 * PITCH, WIDTH)
    wide, wide_back = (
        jnp.pad(wide, ((0, 0), (lo, LANES - 9 * PITCH - lo), (0, 0))) for lo in (12, 12 + STRIP - 1)
    )

    pos = GRID * STRIP
    q, e, c, q_back, c_back, side, upc, downc = pl.pallas_call(
        split_kernel,
        out_shape=(
            sds((5, pos, WIDTH), BF16),
            sds((4, pos, WIDTH), BF16),
            sds((5, pos, WIDTH), BF16),
            sds((5, pos, WIDTH), BF16),
            sds((5, pos, WIDTH), BF16),
            sds((4, GRID * 16, WIDTH), BF16),
            sds((4, MARGIN * 16, WIDTH), BF16),
            sds((4, MARGIN * 16, WIDTH), BF16),
        ),
        in_specs=[sm(), sm(), sm(), vm(), vm(), vm(), vm()],
        out_specs=(vm(),) * 8,
        compiler_params=PARAMS,
    )(owner, labels, mask, perm, earlier, later, cot)

    up_pairs = [(i + 1, i) for i in range(rows - 1)]
    down_pairs = [(i, i + 1) for i in range(rows - 1)]
    cross = [(0, 1), (1, 0)]

    def diagonal(pairs):
        return [(a * cols + x, b * cols + y) for a, b in pairs for x, y in cross]

    def exchange(up, down, side, up_side, down_side):
        return (
            lax.ppermute(down, "rows", down_pairs),
            lax.ppermute(up, "rows", up_pairs),
            lax.ppermute(side, "cols", cross),
            lax.ppermute(down_side, ("rows", "cols"), diagonal(down_pairs)),
            lax.ppermute(up_side, ("rows", "cols"), diagonal(up_pairs)),
        )

    halo = exchange(e[:, : MARGIN * STRIP], e[:, pos - MARGIN * STRIP :], side, upc, downc)
    ext, flow, proj = pl.pallas_call(
        forward_kernel,
        out_shape=(
            sds((5, EXT_ROWS, WIDTH), BF16),
            sds((2, WIDTH, 1024), BF16),
            sds((162, WIDTH), F32),
        ),
        in_specs=[vm()] * 10 + [sm()],
        out_specs=(vm(),) * 3,
        scratch_shapes=[pltpu.VMEM((5, pos, LANES), BF16), pltpu.VMEM((4, pos, WIDTH), BF16), pltpu.VMEM((128, WIDTH), F32)],
        compiler_params=PARAMS,
    )(perm, wide_back, q_back, e, *halo, c_back, left)
    proj = proj + lax.ppermute(proj, "cols", cross)
    distance = 1
    while distance < rows:
        proj = proj + lax.ppermute(proj, "rows", [(i, i ^ distance) for i in range(rows)])
        distance *= 2
    proj = proj * (1.0 / math.sqrt(2 * rows * cols * 1024))
    rim = (4, MARGIN * STRIP, WIDTH)
    corner = (4, MARGIN * 16, WIDTH)
    g_first, centre, *rims = pl.pallas_call(
        backward_kernel,
        out_shape=(
            sds((2, CHANNELS, 1024), BF16),
            sds((4, pos, WIDTH), F32),
            sds(rim, BF16),
            sds(rim, BF16),
            sds((4, GRID * 16, WIDTH), BF16),
            sds(corner, BF16),
            sds(corner, BF16),
        ),
        in_specs=[vm()] * 5 + [sm()] * 2,
        out_specs=(vm(),) * 7,
        scratch_shapes=[
            pltpu.VMEM((5, EXT_ROWS, WIDTH), F32),
            pltpu.VMEM((5, pos, LANES), F32),
            pltpu.VMEM((4, pos, WIDTH), F32),
        ],
        compiler_params=PARAMS,
    )(perm, wide, q, ext, c, left, mask)
    got_above, got_below, got_side, got_above_side, got_below_side = exchange(*rims)
    g_second = pl.pallas_call(
        finish_kernel,
        out_shape=sds((2, CHANNELS, 1024), BF16),
        in_specs=[vm(), sm(), sm()] + [vm()] * 6,
        out_specs=vm(),
        scratch_shapes=[pltpu.VMEM((4, pos, WIDTH), F32)],
        compiler_params=PARAMS,
    )(perm, left, mask, centre, got_above, got_below, got_side, got_above_side, got_below_side)
    return flow, g_first, g_second, proj


def solution(mesh):
    spec = P(("groups", "rows", "cols"), None, None)
    return jax.shard_map(
        shards,
        mesh=mesh,
        in_specs=(spec, spec, spec, P(), P("groups"), P(("groups", "rows", "cols"), None), P(("groups", "rows", "cols"))),
        out_specs=(spec, spec, spec, P("groups", None)),
        check_vma=False,
    )
```
